128 devices in a mesh: dom: 128 (over z, x, y, core).
Axes of the slice: x: 4, y: 4, z: 4, core: 2. Of those that a mesh axis runs over, the one named last changes fastest.
Arguments:
- features: bfloat16 [1048576, 128], P('dom'), may hold values from -5000 to 5000
- teacher_w: bfloat16 [128, 172], replicated, may hold values from -1.5 to 1.5
- teacher_b: float32 [172], replicated, may hold values from -4 to 4
- ema_prior: float32 [172], replicated, may hold values from 0.001 to 0.02
- target_prior: float32 [172], replicated, may hold values from 0.001 to 0.02
- send_rows: int32 [16384, 32], P('dom'), may hold values from 0 to 8191
- send_count: int32 [16384], P('dom'), may hold values from 16 to 32, as said below
- tiles: bfloat16 [8192, 8, 128, 128], P('dom'), as said below
- tile_col: int32 [8192, 8], P('dom'), may hold values from 0 to 95
- tile_count: int32 [8192], P('dom'), may hold values from 2 to 8, as said below
Outputs:
- log_scores: float32 [1048576, 172], P('dom')
The draws below stay inside these ranges and needn't reach their ends.
Inputs may be any that keep to these rules, and one draw needn't show every extreme that they name: `send_count`: at most 32 slots are used from one partition to another; in every draw some partition receives 32 rows from every partition. `tile_count`: in every partition some row block uses all 8 slots. `tiles`: Nonnegative.
All inputs are finite; a program needn't handle non-finite values.
Results may differ from the reference program's by a relative error of at most 0.00085.
Values may be sent and summed in bfloat16 or wider, within the bound.
A program may use at most 128 MiB of HBM per device.

```python
import math
import jax
import jax.numpy as jnp
from jax import lax

F = 128
C = 172
B = 128
RB = 64
TPR = 8
SLOT = 32
STEPS = 3
ROWS = 8192
HB = 32
NODES = 1048576
N_DOM = 128


def draw_features(key, part):
    base = jnp.clip(jax.random.normal(jax.random.fold_in(key, 11), (N_DOM, ROWS, F), jnp.float32), -6.0, 6.0)
    topic = jnp.clip(jax.random.normal(jax.random.fold_in(key, 12), (N_DOM, 1, F), jnp.float32), -6.0, 6.0)
    rising = 0.5 + jnp.arange(N_DOM).astype(jnp.float32)[:, None, None] / max(N_DOM - 1, 1)
    era_table = jnp.clip(jax.random.normal(jax.random.fold_in(key, 15), (8, F), jnp.float32), -6.0, 6.0)
    cycle_table = jnp.clip(jax.random.normal(jax.random.fold_in(key, 16), (16, F), jnp.float32), -6.0, 6.0)
    row_ids = jnp.arange(ROWS).astype(jnp.int32)
    era_ids = jnp.minimum(row_ids // max(ROWS // 8, 1), 7)
    cycle_ids = row_ids % 16
    shared = era_table[era_ids] + cycle_table[cycle_ids]
    values = 0.7 * base + 0.7 * rising * topic + 0.7 * shared[None, :, :]
    return values.reshape(NODES, F).astype(jnp.bfloat16)


def draw_send_count(key, part):
    counts = jax.random.randint(jax.random.fold_in(key, 21), (N_DOM, N_DOM), (SLOT + 1) // 2, SLOT + 1)
    full_target = jax.random.randint(jax.random.fold_in(key, 22), (), 0, N_DOM)
    counts = jnp.where(jnp.arange(N_DOM)[None, :] == full_target, SLOT, counts)
    return counts.reshape(N_DOM * N_DOM).astype(jnp.int32)


def count_table(key):
    ceiling = jax.random.randint(jax.random.fold_in(key, 51), (N_DOM, 1), 2, TPR + 1)
    counts = jax.random.randint(jax.random.fold_in(key, 52), (N_DOM, RB), 2, ceiling + 1)
    return jnp.where(jnp.arange(RB)[None, :] == 0, TPR, counts)


def draw_tiles(key, part):
    density = min(6.0 / B, 0.5)
    counts = count_table(key).astype(jnp.float32).reshape(N_DOM * RB, 1, 1, 1)
    hits = jax.random.uniform(jax.random.fold_in(key, 31), (N_DOM * RB, TPR, B, B), jnp.float32) < density
    weights = jax.random.uniform(jax.random.fold_in(key, 32), (N_DOM * RB, TPR, B, B), jnp.float32, 0.5, 1.5)
    values = jnp.where(hits, weights, 0.0) / (counts * (B * density))
    return values.astype(jnp.bfloat16)


def draw_tile_col(key, part):
    random_cols = jax.random.randint(jax.random.fold_in(key, 41), (N_DOM, RB, TPR), 0, RB + HB)
    block_row = jnp.arange(RB)[None, :, None]
    slot_pos = jnp.arange(TPR)[None, None, :]
    boundary_cols = RB + (2 * block_row + slot_pos) % HB
    columns = jnp.where(slot_pos < 2, boundary_cols, random_cols)
    return columns.reshape(N_DOM * RB, TPR).astype(jnp.int32)


def draw_tile_count(key, part):
    return count_table(key).reshape(N_DOM * RB).astype(jnp.int32)


def plant(entries, rng, smallest, top_value):
    longest = entries.shape.index(max(entries.shape))
    spots = []
    for shift in (0, 1):
        where = [jax.random.randint(jax.random.fold_in(rng, axis), (), 0, length) for axis, length in enumerate(entries.shape)]
        where[longest] = (where[longest] + shift) % entries.shape[longest]
        spots.append(tuple(where))
    return entries.at[spots[0]].set(smallest).at[spots[1]].set(top_value)


def bell_draw(rng, shape, deviation, most, held_as=jnp.bfloat16):
    array = jax.random.normal(rng, shape, jnp.float32) * deviation
    return jnp.minimum(jnp.maximum(array, -most), most).astype(held_as)


def setup_inputs(seed: int = 0) -> dict:
    keys = jax.random.split(jax.random.key(seed), 11)
    features = draw_features(jax.random.fold_in(keys[10], 71), 0)
    teacher_w = bell_draw(keys[1], (F, C), (F // 9) ** -0.5, 1.5)
    teacher_b = bell_draw(keys[2], (C,), 1.0, 4.0, jnp.float32)
    ema_prior = jnp.clip(jnp.exp(jax.random.uniform(keys[3], (C,), jnp.float32, math.log(0.001), math.log(0.02))), 0.001, 0.02)
    target_prior = jnp.clip(jnp.exp(jax.random.uniform(keys[4], (C,), jnp.float32, math.log(0.001), math.log(0.02))), 0.001, 0.02)
    send_rows = plant(jax.random.randint(keys[5], (N_DOM * N_DOM, SLOT), 0, ROWS), jax.random.fold_in(keys[5], 1), 0, ROWS - 1).astype(jnp.int32)
    send_count = draw_send_count(jax.random.fold_in(keys[10], 71), 0)
    tiles = draw_tiles(jax.random.fold_in(keys[10], 71), 0)
    tile_col = draw_tile_col(jax.random.fold_in(keys[10], 71), 0)
    tile_count = draw_tile_count(jax.random.fold_in(keys[10], 71), 0)
    return dict(features=features, teacher_w=teacher_w, teacher_b=teacher_b, ema_prior=ema_prior, target_prior=target_prior, send_rows=send_rows, send_count=send_count, tiles=tiles, tile_col=tile_col, tile_count=tile_count)


MOMENTUM = 0.7
PROPAGATE = 0.9
LOG_FLOOR = 1e-4


def reference(features, teacher_w, teacher_b, ema_prior, target_prior, send_rows, send_count, tiles, tile_col, tile_count):
    logits = jnp.dot(features, teacher_w, preferred_element_type=jnp.float32) + teacher_b
    class_probs = jax.nn.softmax(logits, axis=-1).astype(jnp.bfloat16)
    batch_marginal = jnp.sum(class_probs.astype(jnp.float32), axis=0)
    marginal = MOMENTUM * ema_prior + (1.0 - MOMENTUM) * batch_marginal / NODES
    ratio = target_prior / marginal
    scaled = class_probs.astype(jnp.float32) * ratio
    seed_labels = scaled / jnp.sum(scaled, axis=-1, keepdims=True)
    seed_parts = seed_labels.reshape(N_DOM, ROWS, C)
    route_rows = send_rows.reshape(N_DOM, N_DOM, SLOT)
    route_count = send_count.reshape(N_DOM, N_DOM)
    tile_parts = tiles.reshape(N_DOM, RB, TPR, B, B)
    column_parts = tile_col.reshape(N_DOM, RB, TPR)
    count_parts = tile_count.reshape(N_DOM, RB)
    sources = jnp.arange(N_DOM).astype(jnp.int32)
    slot_index = jnp.arange(SLOT).astype(jnp.int32)
    tile_index = jnp.arange(TPR).astype(jnp.int32)
    current = seed_parts
    for sweep in range(STEPS):
        labels = current.astype(jnp.bfloat16)

        def device_step(target):
            picks = route_rows[:, target, :]
            far_rows = labels[sources[:, None], picks]
            alive = slot_index[None, :] < route_count[:, target][:, None]
            far_rows = jnp.where(alive[:, :, None], far_rows, jnp.zeros((), jnp.bfloat16))
            blocks = jnp.concatenate([labels[target].reshape(RB, B, C), far_rows.reshape(HB, B, C)], axis=0)
            picked = blocks[column_parts[target]]
            used = tile_index[None, :] < count_parts[target][:, None]
            live_tiles = jnp.where(used[:, :, None, None], tile_parts[target], jnp.zeros((), jnp.bfloat16))
            mixed_sum = jnp.einsum("rtij,rtjc->ric", live_tiles.astype(jnp.float32), picked.astype(jnp.float32))
            return mixed_sum.reshape(ROWS, C)

        gathered = lax.map(device_step, sources)
        current = PROPAGATE * gathered + (1.0 - PROPAGATE) * seed_parts
    return jnp.log(current + LOG_FLOOR).reshape(NODES, C)
```

```python
import functools

import jax
import jax.numpy as jnp
from jax import lax
from jax.experimental import pallas as pl
from jax.experimental.pallas import tpu as pltpu
from jax.sharding import PartitionSpec as P

F = 128
C = 172
CP = 256
B = 128
RB = 64
TPR = 8
SLOT = 32
PACK = 48
HB = 32
ROWS = 8192
N = 128
NODES = ROWS * N

MOMENTUM = 0.7
PROPAGATE = 0.9
LOG_FLOOR = 0.0001
DEAD = 32768.0
LOW = -1e30
MESH = pl.DeviceIdType.MESH
MIX = 37
GROUP = 16
F32 = jnp.float32
BF16 = jnp.bfloat16


def full_vmem():
    return pl.BlockSpec(memory_space=pltpu.VMEM)


def full_smem():
    return pl.BlockSpec(memory_space=pltpu.SMEM)


def greet(me):
    barrier = pltpu.get_barrier_semaphore()

    def tell(k, carry):
        other = lax.rem(me + k, N)
        pl.semaphore_signal(barrier, inc=1, device_id=(other,), device_id_type=MESH)
        return carry

    lax.fori_loop(1, N, tell, 0)
    return barrier


def softmax_rows(feats, wt, bias):
    logits = lax.dot_general(feats, wt, (((1,), (1,)), ((), ())), preferred_element_type=F32) + bias
    top = jnp.max(logits, axis=-1, keepdims=True)
    e = jnp.exp(logits - top)
    return (e / jnp.sum(e, axis=-1, keepdims=True)).astype(BF16)


def fill_teacher(wt_ref, b_ref, wpad, bpad):
    wpad[...] = jnp.zeros_like(wpad)
    wpad[pl.ds(0, C), :] = wt_ref[...].astype(F32)
    bpad[...] = jnp.full(bpad.shape, LOW, F32)
    bpad[:, pl.ds(0, C)] = b_ref[...]


def teacher_kernel(
    rows_ref, cnt_ref, feat_ref, wt_ref, b_ref,
    probs_ref, recv_ref, total_ref,
    feat32, stage, sendbuf, wpad, bpad, part1, part2,
    send_sem, recv_sem, send1, recv1, send2, recv2,
):
    me = lax.axis_index("dom")
    barrier = greet(me)

    def widen(k, carry):
        at = pl.multiple_of(k * 256, 256)
        feat32[pl.ds(at, 256), :] = feat_ref[pl.ds(at, 256), :].astype(F32)
        return carry

    lax.fori_loop(0, ROWS // 256, widen, 0)
    fill_teacher(wt_ref, b_ref, wpad, bpad)

    def gather(dest):
        for j in range(SLOT):
            stage[pl.ds(j, 1), :] = feat32[pl.ds(rows_ref[j, dest], 1), :]
        live = lax.broadcasted_iota(jnp.int32, (SLOT, F), 0) < cnt_ref[dest]
        return jnp.where(live, stage[...], DEAD).astype(BF16)

    recv_ref[pl.ds(me, 1)] = gather(me)[None]
    pl.semaphore_wait(barrier, N - 1)

    def send(k, carry):
        dest = lax.rem(me + lax.rem(k * MIX, N), N)
        sendbuf[pl.ds(k, 1)] = gather(dest)[None]
        pltpu.make_async_remote_copy(
            src_ref=sendbuf.at[k], dst_ref=recv_ref.at[me], send_sem=send_sem, recv_sem=recv_sem,
            device_id=(dest,), device_id_type=MESH,
        ).start()
        return carry

    lax.fori_loop(1, N, send, 0)

    wt = wpad[...].astype(BF16)
    bias = bpad[...]

    def local(k, acc):
        at = pl.multiple_of(k * 256, 256)
        p = softmax_rows(feat_ref[pl.ds(at, 256), :], wt, bias)
        probs_ref[pl.ds(at, 256), :] = p
        return acc + jnp.sum(p.astype(F32).reshape(32, 8, CP), axis=0)

    acc = lax.fori_loop(0, ROWS // 256, local, jnp.zeros((8, CP), F32))

    group = me // GROUP
    place = lax.rem(me, GROUP)
    part1[pl.ds(place, 1)] = acc[None]

    def send_near(k, carry):
        other = group * GROUP + lax.rem(place + k, GROUP)
        pltpu.make_async_remote_copy(
            src_ref=part1.at[place], dst_ref=part1.at[place], send_sem=send1, recv_sem=recv1,
            device_id=(other,), device_id_type=MESH,
        ).start()
        return carry

    lax.fori_loop(1, GROUP, send_near, 0)
    near = pltpu.make_async_remote_copy(
        src_ref=part1.at[pl.ds(0, GROUP - 1)], dst_ref=part1.at[pl.ds(0, GROUP - 1)], send_sem=send1, recv_sem=recv1,
        device_id=(lax.rem(me + 1, N),), device_id_type=MESH,
    )
    near.wait_recv()
    part2[pl.ds(group, 1)] = jnp.sum(part1[...], axis=0)[None]

    groups = N // GROUP

    def send_far(k, carry):
        other = lax.rem(group + k, groups) * GROUP + place
        pltpu.make_async_remote_copy(
            src_ref=part2.at[group], dst_ref=part2.at[group], send_sem=send2, recv_sem=recv2,
            device_id=(other,), device_id_type=MESH,
        ).start()
        return carry

    lax.fori_loop(1, groups, send_far, 0)
    far = pltpu.make_async_remote_copy(
        src_ref=part2.at[pl.ds(0, groups - 1)], dst_ref=part2.at[pl.ds(0, groups - 1)], send_sem=send2, recv_sem=recv2,
        device_id=(lax.rem(me + 1, N),), device_id_type=MESH,
    )
    far.wait_recv()
    total_ref[...] = jnp.sum(part2[...], axis=0)
    near.wait_send()
    far.wait_send()
    bulk = pltpu.make_async_remote_copy(
        src_ref=sendbuf.at[pl.ds(0, N - 1)], dst_ref=recv_ref.at[pl.ds(0, N - 1)], send_sem=send_sem, recv_sem=recv_sem,
        device_id=(lax.rem(me + 1, N),), device_id_type=MESH,
    )
    bulk.wait_recv()
    bulk.wait_send()


def teacher(rows_t, counts, features, wt, bias):
    return pl.pallas_call(
        teacher_kernel,
        out_shape=(
            jax.ShapeDtypeStruct((ROWS, CP), BF16),
            jax.ShapeDtypeStruct((N, SLOT, F), BF16),
            jax.ShapeDtypeStruct((8, CP), F32),
        ),
        in_specs=[full_smem(), full_smem(), full_vmem(), full_vmem(), full_vmem()],
        out_specs=(full_vmem(), full_vmem(), full_vmem()),
        scratch_shapes=[
            pltpu.VMEM((ROWS, F), F32),
            pltpu.VMEM((SLOT, F), F32),
            pltpu.VMEM((N, SLOT, F), BF16),
            pltpu.VMEM((CP, F), F32),
            pltpu.VMEM((1, CP), F32),
            pltpu.VMEM((GROUP, 8, CP), F32),
            pltpu.VMEM((N // GROUP, 8, CP), F32),
        ] + [pltpu.SemaphoreType.DMA] * 6,
        compiler_params=pltpu.CompilerParams(collective_id=0, has_side_effects=True, vmem_limit_bytes=40 * 2**20),
        cost_estimate=pl.CostEstimate(flops=2 * ROWS * F * CP, bytes_accessed=8 * 2**20, transcendentals=ROWS * CP),
        name="teacher",
    )(rows_t, counts, features, wt, bias)


def exchange_kernel(rows_ref, cnt_ref, labels_ref, recv_ref, wide, stage, sendbuf, send_sem, recv_sem):
    me = lax.axis_index("dom")
    barrier = greet(me)

    def widen(k, carry):
        at = pl.multiple_of(k * 128, 128)
        wide[pl.ds(at, 128), :] = labels_ref[pl.ds(at, 128), :].astype(F32)
        return carry

    lax.fori_loop(0, ROWS // 128, widen, 0)

    def gather(dest):
        for j in range(SLOT):
            stage[pl.ds(j, 1), :] = wide[pl.ds(rows_ref[j, dest], 1), :]
        live = lax.broadcasted_iota(jnp.int32, (SLOT, CP), 0) < cnt_ref[dest]
        rows = jnp.where(live, stage[...], 0.0)
        high = rows[:, F:]
        lane = lax.broadcasted_iota(jnp.int32, (SLOT // 2, F), 1)
        high = jnp.where(lane < F // 2, high[: SLOT // 2], pltpu.roll(high[SLOT // 2 :], F // 2, 1))
        return jnp.concatenate([rows[:, :F], high], axis=0).astype(BF16)

    recv_ref[pl.ds(me, 1)] = gather(me)[None]
    pl.semaphore_wait(barrier, N - 1)

    def send(k, carry):
        dest = lax.rem(me + lax.rem(k * MIX, N), N)
        sendbuf[pl.ds(k, 1)] = gather(dest)[None]
        pltpu.make_async_remote_copy(
            src_ref=sendbuf.at[k], dst_ref=recv_ref.at[me], send_sem=send_sem, recv_sem=recv_sem,
            device_id=(dest,), device_id_type=MESH,
        ).start()
        return carry

    lax.fori_loop(1, N, send, 0)
    bulk = pltpu.make_async_remote_copy(
        src_ref=sendbuf.at[pl.ds(0, N - 1)], dst_ref=recv_ref.at[pl.ds(0, N - 1)], send_sem=send_sem, recv_sem=recv_sem,
        device_id=(lax.rem(me + 1, N),), device_id_type=MESH,
    )
    bulk.wait_recv()
    bulk.wait_send()


def exchange(rows_t, counts, labels, number):
    return pl.pallas_call(
        exchange_kernel,
        out_shape=jax.ShapeDtypeStruct((N, PACK, F), BF16),
        in_specs=[full_smem(), full_smem(), full_vmem()],
        out_specs=full_vmem(),
        scratch_shapes=[
            pltpu.VMEM((ROWS, CP), F32),
            pltpu.VMEM((SLOT, CP), F32),
            pltpu.VMEM((N, PACK, F), BF16),
        ] + [pltpu.SemaphoreType.DMA] * 2,
        compiler_params=pltpu.CompilerParams(collective_id=number, has_side_effects=True, vmem_limit_bytes=40 * 2**20),
        cost_estimate=pl.CostEstimate(flops=0, bytes_accessed=8 * 2**20, transcendentals=0),
        name="exchange",
    )(rows_t, counts, labels)


PER = 4


def products(r, tiles_ref, local_r, col_ref, count_ref, labels, acc_ref):
    count = count_ref[r]
    cols = [jnp.where(t < count, col_ref[t, r], RB + HB) for t in range(TPR)]
    for pairs in range(1, TPR // 2 + 1):
        here = (count + 1) // 2 == pairs if pairs > 1 else count <= 2

        @pl.when(here)
        def _():
            lhs = jnp.concatenate([tiles_ref[local_r, t] for t in range(2 * pairs)], axis=1)
            rhs = jnp.concatenate([labels[cols[t]] for t in range(2 * pairs)], axis=0)
            acc_ref[...] = jnp.dot(lhs, rhs, preferred_element_type=F32)


def first_kernel(
    count_ref, col_ref, tiles_ref, probs_hbm, feats_ref, total_ref, ema_ref, target_ref, wt_ref, b_ref,
    seed_ref, out_ref,
    labels, feats, acc_ref, wpad, bpad, ratio_ref, ema, target, sem,
):
    step = pl.program_id(0)

    @pl.when(step == 0)
    def _():
        copy = pltpu.make_async_copy(probs_hbm, labels.at[pl.ds(0, RB)], sem)
        copy.start()
        fill_teacher(wt_ref, b_ref, wpad, bpad)
        ema[...] = jnp.full(ema.shape, 1.0, F32)
        ema[:, pl.ds(0, C)] = ema_ref[...]
        target[...] = jnp.zeros_like(target)
        target[:, pl.ds(0, C)] = target_ref[...]
        total = jnp.sum(total_ref[...], axis=0, keepdims=True)
        marginal = MOMENTUM * ema[...] + (1.0 - MOMENTUM) * total / NODES
        ratio_ref[...] = target[...] / marginal
        labels[pl.ds(RB + HB, 1)] = jnp.zeros((1, B, CP), BF16)
        wt = wpad[...].astype(BF16)
        bias = bpad[...]
        ratio = ratio_ref[...]

        def align(p):
            scaled = p.astype(F32) * ratio
            row_total = jnp.sum(scaled, axis=-1, keepdims=True)
            return scaled / jnp.where(row_total > 0.0, row_total, 1.0)

        def far(h, carry):
            f = feats_ref[pl.ds(pl.multiple_of(h * B, B), B), :]
            live = jnp.broadcast_to(f[:, :1].astype(F32) < DEAD / 2, (B, CP))
            p = softmax_rows(f, wt, bias)
            labels[pl.ds(RB + h, 1)] = jnp.where(live, align(p), 0.0).astype(BF16)[None]
            return carry

        lax.fori_loop(0, HB, far, 0)
        copy.wait()

        def near(r, carry):
            labels[pl.ds(r, 1)] = align(labels[r]).astype(BF16)[None]
            return carry

        lax.fori_loop(0, RB, near, 0)

    def block(i, carry):
        r = step * PER + i
        products(r, tiles_ref, i, col_ref, count_ref, labels, acc_ref)
        seed = labels[r]
        seed_ref[pl.ds(i, 1)] = seed[None]
        out_ref[pl.ds(i, 1)] = (PROPAGATE * acc_ref[...] + (1.0 - PROPAGATE) * seed.astype(F32)).astype(BF16)[None]
        return carry

    lax.fori_loop(0, PER, block, 0)


def later_kernel(last, count_ref, col_ref, tiles_ref, labels_hbm, far_ref, seed_ref, out_ref, labels, acc_ref, sem):
    step = pl.program_id(0)

    @pl.when(step == 0)
    def _():
        copy = pltpu.make_async_copy(labels_hbm, labels.at[pl.ds(0, RB)], sem)
        copy.start()
        labels[pl.ds(RB + HB, 1)] = jnp.zeros((1, B, CP), BF16)

        def far(h, carry):
            lane = lax.broadcasted_iota(jnp.int32, (SLOT // 2, F), 1)
            for s in range(B // SLOT):
                packed = far_ref[h * (B // SLOT) + s].astype(F32)
                high = packed[SLOT:]
                other = pltpu.roll(high, F // 2, 1)
                high = jnp.concatenate([high, other], axis=0)
                lane = lax.broadcasted_iota(jnp.int32, (SLOT, F), 1)
                high = jnp.where(lane < F // 2, high, 0.0)
                rows = jnp.concatenate([packed[:SLOT], high], axis=1).astype(BF16)
                labels[pl.ds(RB + h, 1), pl.ds(s * SLOT, SLOT), :] = rows[None]
            return carry

        lax.fori_loop(0, HB, far, 0)
        copy.wait()

    def block(i, carry):
        r = step * PER + i
        products(r, tiles_ref, i, col_ref, count_ref, labels, acc_ref)
        current = PROPAGATE * acc_ref[...] + (1.0 - PROPAGATE) * seed_ref[i].astype(F32)
        if last:
            flipped = current.T[:C]
            out_ref[:, pl.ds(pl.multiple_of(i * B, B), B)] = jnp.log(flipped + LOG_FLOOR)
        else:
            out_ref[pl.ds(i, 1)] = current.astype(BF16)[None]
        return carry

    lax.fori_loop(0, PER, block, 0)


def tile_spec():
    return pl.BlockSpec((PER, TPR, B, B), lambda i: (i, 0, 0, 0))


def label_spec():
    return pl.BlockSpec((PER, B, CP), lambda i: (i, 0, 0))


PRODUCT_COST = pl.CostEstimate(flops=2 * RB * TPR * B * B * CP, bytes_accessed=28 * 2**20, transcendentals=0)


def first_step(counts, cols_t, tiles, probs, feats, total, ema, target, wt, bias):
    shape = jax.ShapeDtypeStruct((RB, B, CP), BF16)
    return pl.pallas_call(
        first_kernel,
        grid=(RB // PER,),
        out_shape=(shape, shape),
        in_specs=[full_smem(), full_smem(), tile_spec(), pl.BlockSpec(memory_space=pl.ANY)] + [full_vmem()] * 6,
        out_specs=(label_spec(), label_spec()),
        scratch_shapes=[
            pltpu.VMEM((RB + HB + 1, B, CP), BF16),
            pltpu.VMEM((8, F), BF16),
            pltpu.VMEM((B, CP), F32),
            pltpu.VMEM((CP, F), F32),
            pltpu.VMEM((1, CP), F32),
            pltpu.VMEM((1, CP), F32),
            pltpu.VMEM((1, CP), F32),
            pltpu.VMEM((1, CP), F32),
            pltpu.SemaphoreType.DMA,
        ],
        compiler_params=pltpu.CompilerParams(vmem_limit_bytes=40 * 2**20),
        cost_estimate=PRODUCT_COST,
        name="first_step",
    )(counts, cols_t, tiles, probs.reshape(RB, B, CP), feats.reshape(HB * B, F), total, ema, target, wt, bias)


def later_step(last, counts, cols_t, tiles, labels, far, seed):
    if last:
        shape = jax.ShapeDtypeStruct((C, ROWS), F32)
        spec = pl.BlockSpec((C, PER * B), lambda i: (0, i))
    else:
        shape = jax.ShapeDtypeStruct((RB, B, CP), BF16)
        spec = label_spec()
    return pl.pallas_call(
        functools.partial(later_kernel, last),
        grid=(RB // PER,),
        out_shape=shape,
        in_specs=[full_smem(), full_smem(), tile_spec(), pl.BlockSpec(memory_space=pl.ANY), full_vmem(), label_spec()],
        out_specs=spec,
        scratch_shapes=[
            pltpu.VMEM((RB + HB + 1, B, CP), BF16),
            pltpu.VMEM((B, CP), F32),
            pltpu.SemaphoreType.DMA,
        ],
        compiler_params=pltpu.CompilerParams(vmem_limit_bytes=40 * 2**20),
        cost_estimate=PRODUCT_COST,
        name="last_step" if last else "later_step",
    )(counts, cols_t, tiles, labels, far, seed)


def on_device(
    features, teacher_w, teacher_b, ema_prior, target_prior, send_rows, send_count, tiles, tile_col, tile_count
):
    rows_t = send_rows.T
    cols_t = tile_col.T
    wt = teacher_w.T
    bias = teacher_b.reshape(1, C)
    probs, feats, total = teacher(rows_t, send_count, features, wt, bias)
    seed, labels = first_step(
        tile_count, cols_t, tiles, probs, feats, total, ema_prior.reshape(1, C), target_prior.reshape(1, C), wt, bias
    )
    far = exchange(rows_t, send_count, labels.reshape(ROWS, CP), 1)
    labels = later_step(False, tile_count, cols_t, tiles, labels, far, seed)
    far = exchange(rows_t, send_count, labels.reshape(ROWS, CP), 2)
    out_t = later_step(True, tile_count, cols_t, tiles, labels, far, seed)
    return out_t.T


def solution(mesh):
    placed = (
        P("dom", None), P(), P(), P(), P(), P("dom", None), P("dom"),
        P("dom", None, None, None), P("dom", None), P("dom"),
    )
    return jax.shard_map(on_device, mesh=mesh, in_specs=placed, out_specs=P("dom", None), check_vma=False)
```

```python
import jax
import jax.numpy as jnp
from jax import lax
from jax.experimental import pallas as pl
from jax.experimental.pallas import tpu as pltpu
from jax.sharding import PartitionSpec as P

F = 128
C = 172
CP = 256
B = 128
RB = 64
TPR = 8
SLOT = 32
HALF = 128
PACK = 16
CHUNK = 1024
UNROLL = 8
HB = 32
ROWS = 8192
N = 128
NODES = ROWS * N

MOMENTUM = 0.7
PROPAGATE = 0.9
LOG_FLOOR = 0.0001
DEAD = 32768.0
LOW = -1e30
VMEM_LIMIT = 56 * 2**20
MESH = pl.DeviceIdType.MESH
MIX = 37
GROUP = 16
F32 = jnp.float32
BF16 = jnp.bfloat16


def in_hbm():
    return pl.BlockSpec(memory_space=pltpu.HBM)


def in_vmem():
    return pl.BlockSpec(memory_space=pltpu.VMEM)


def propagate_kernel(
    rows_hbm, cnt_hbm, feat_hbm, wt_hbm, b_hbm, ema_hbm, target_hbm, tiles_hbm, col_hbm, used_hbm,
    wide_a, wide_b,
    rows_v, rows_w, rows, cnt, feat, wt, bias, ema, target, tiles, col, used,
    wpad, bpad, epad, tpad, stage,
    seed_a, seed_b, one_a, one_b, two_a, two_b,
    feat_send, feat_recv, send_a1, send_a2, send_b1, send_b2, recv_b1, recv_b2,
    part1, part2, load_sem, flip_sem, send_sem, recv_sem,
):
    me = lax.axis_index("dom")
    next_door = lax.rem(me + 1, N)

    loads = [
        pltpu.make_async_copy(src, dst, load_sem.at[i])
        for i, (src, dst) in enumerate(
            (
                (rows_hbm, rows_v), (feat_hbm, feat), (cnt_hbm, cnt), (wt_hbm, wt), (b_hbm, bias), (ema_hbm, ema),
                (target_hbm, target), (col_hbm, col), (used_hbm, used), (tiles_hbm, tiles),
            )
        )
    ]
    for load in loads:
        load.start()

    barrier = pltpu.get_barrier_semaphore()

    def tell(k, carry):
        pl.semaphore_signal(barrier, inc=1, device_id=(lax.rem(me + k, N),), device_id_type=MESH)
        return carry

    lax.fori_loop(1, N, tell, 0)

    loads[0].wait()
    rows_w[...] = jnp.concatenate([rows_v[...], jnp.zeros((B - SLOT, N), jnp.int32)], axis=0).T
    flip = pltpu.make_async_copy(rows_w, rows, flip_sem)
    flip.start()
    loads[1].wait()

    def widen(k, carry):
        at = pl.multiple_of(k * CHUNK, CHUNK)
        wide_a[pl.ds(at, CHUNK), :] = feat[pl.ds(at, CHUNK), :].astype(F32)
        return carry

    lax.fori_loop(0, ROWS // CHUNK, widen, 0)
    for load in loads[2:9]:
        load.wait()
    flip.wait()

    def picked(wide, dest, dead):
        for j in range(SLOT):
            stage[pl.ds(j, 1), :] = wide[pl.ds(rows[dest, j], 1), :]
        live = lax.broadcasted_iota(jnp.int32, (SLOT, HALF), 0) < cnt[dest]
        return jnp.where(live, stage[...], dead)

    def packed(values):
        lane = lax.broadcasted_iota(jnp.int32, (PACK, HALF), 1)
        return jnp.where(lane < HALF // 2, values[:PACK], pltpu.roll(values[PACK:], HALF // 2, 1))

    def spread(make, sendbuf, landing, number):
        def send(k, carry):
            dest = lax.rem(me + lax.rem(k * MIX, N), N)
            sendbuf[pl.ds(k, 1)] = make(dest)[None]
            pltpu.make_async_remote_copy(
                src_ref=sendbuf.at[k], dst_ref=landing, send_sem=send_sem.at[number], recv_sem=recv_sem.at[number],
                device_id=(dest,), device_id_type=MESH,
            ).start()
            return carry

        lax.fori_loop(1, N, send, 0)
        whole = sendbuf.at[pl.ds(0, N - 1)]
        return pltpu.make_async_remote_copy(
            src_ref=whole, dst_ref=whole, send_sem=send_sem.at[number], recv_sem=recv_sem.at[number],
            device_id=(next_door,), device_id_type=MESH,
        )

    block_me = RB + me // (B // SLOT)
    row_me = pl.multiple_of(lax.rem(me, B // SLOT) * SLOT, SLOT)

    def own_place(labels):
        return labels.at[block_me, pl.ds(row_me, SLOT), :]

    def put_own(labels, values):
        labels[pl.ds(block_me, 1), pl.ds(row_me, SLOT), :] = values[None]

    def feature_rows(dest):
        return picked(wide_a, dest, DEAD).astype(BF16)

    def rows_a(dest):
        return picked(wide_a, dest, 0.0).astype(BF16)

    def rows_b(dest):
        return packed(picked(wide_b, dest, 0.0)).astype(BF16)

    feat_recv[pl.ds(me, 1)] = feature_rows(me)[None]
    pl.semaphore_wait(barrier, N - 1)
    features_sent = spread(feature_rows, feat_send, feat_recv.at[me], 0)

    wpad[...] = jnp.zeros_like(wpad)
    wpad[pl.ds(0, C), :] = wt[...].astype(F32)
    bpad[...] = jnp.full(bpad.shape, LOW, F32)
    bpad[:, pl.ds(0, C)] = bias[...]
    epad[...] = jnp.full(epad.shape, 1.0, F32)
    epad[:, pl.ds(0, C)] = ema[...]
    tpad[...] = jnp.zeros_like(tpad)
    tpad[:, pl.ds(0, C)] = target[...]
    weights = wpad[...].astype(BF16)
    blocks = CHUNK // B

    def soft(values):
        logits = lax.dot_general(values, weights, (((1,), (1,)), ((), ())), preferred_element_type=F32) + bpad[...]
        e = jnp.exp(logits - jnp.max(logits, axis=-1, keepdims=True))
        return e * (1.0 / jnp.sum(e, axis=-1, keepdims=True))

    def keep(first, values):
        seed_a[pl.ds(first, blocks)] = values[:, :HALF].reshape(blocks, B, HALF)
        seed_b[pl.ds(first, blocks)] = values[:, HALF:].reshape(blocks, B, HALF)

    def local(k, acc):
        p = soft(feat[pl.ds(pl.multiple_of(k * CHUNK, CHUNK), CHUNK), :]).astype(BF16)
        keep(k * blocks, p)
        return acc + jnp.sum(p.astype(F32).reshape(CHUNK // 8, 8, CP), axis=0)

    acc = lax.fori_loop(0, ROWS // CHUNK, local, jnp.zeros((8, CP), F32))

    group = me // GROUP
    place = lax.rem(me, GROUP)
    groups = N // GROUP
    part1[pl.ds(place, 1)] = acc[None]

    def send_near(k, carry):
        pltpu.make_async_remote_copy(
            src_ref=part1.at[place], dst_ref=part1.at[place], send_sem=send_sem.at[5], recv_sem=recv_sem.at[5],
            device_id=(group * GROUP + lax.rem(place + k, GROUP),), device_id_type=MESH,
        ).start()
        return carry

    lax.fori_loop(1, GROUP, send_near, 0)
    near = pltpu.make_async_remote_copy(
        src_ref=part1.at[pl.ds(0, GROUP - 1)], dst_ref=part1.at[pl.ds(0, GROUP - 1)],
        send_sem=send_sem.at[5], recv_sem=recv_sem.at[5], device_id=(next_door,), device_id_type=MESH,
    )
    near.wait_recv()
    part2[pl.ds(group, 1)] = jnp.sum(part1[...], axis=0)[None]

    def send_far(k, carry):
        pltpu.make_async_remote_copy(
            src_ref=part2.at[group], dst_ref=part2.at[group], send_sem=send_sem.at[6], recv_sem=recv_sem.at[6],
            device_id=(lax.rem(group + k, groups) * GROUP + place,), device_id_type=MESH,
        ).start()
        return carry

    lax.fori_loop(1, groups, send_far, 0)
    far = pltpu.make_async_remote_copy(
        src_ref=part2.at[pl.ds(0, groups - 1)], dst_ref=part2.at[pl.ds(0, groups - 1)],
        send_sem=send_sem.at[6], recv_sem=recv_sem.at[6], device_id=(next_door,), device_id_type=MESH,
    )

    features_sent.wait_recv()
    sources = CHUNK // SLOT

    def boundary(k, carry):
        f = feat_recv[pl.ds(k * sources, sources)].reshape(CHUNK, F)
        live = f[:, :1].astype(F32) < DEAD / 2
        keep(RB + k * blocks, jnp.where(live, soft(f), 0.0).astype(BF16))
        return carry

    lax.fori_loop(0, HB * B // CHUNK, boundary, 0)
    far.wait_recv()
    total = jnp.sum(jnp.sum(part2[...], axis=0), axis=0, keepdims=True)
    ratio = tpad[...] / (MOMENTUM * epad[...] + (1.0 - MOMENTUM) * total / NODES)

    def align(k, carry):
        a = seed_a[pl.ds(k * blocks, blocks)].reshape(CHUNK, HALF).astype(F32) * ratio[:, :HALF]
        b = seed_b[pl.ds(k * blocks, blocks)].reshape(CHUNK, HALF).astype(F32) * ratio[:, HALF:]
        row_total = jnp.sum(a + b, axis=-1, keepdims=True)
        scale = 1.0 / jnp.where(row_total > 0.0, row_total, 1.0)
        seed_a[pl.ds(k * blocks, blocks)] = (a * scale).astype(BF16).reshape(blocks, B, HALF)
        seed_b[pl.ds(k * blocks, blocks)] = (b * scale).astype(BF16).reshape(blocks, B, HALF)
        return carry

    lax.fori_loop(0, (RB + HB) * B // CHUNK, align, 0)
    for labels in (seed_a, seed_b, one_a, one_b, two_a, two_b):
        labels[pl.ds(RB + HB, 1)] = jnp.zeros((1, B, HALF), BF16)
    loads[9].wait()

    def multiply(labels, seed, following, wide):
        def several(i, carry):
            for u in range(UNROLL):
                r = i * UNROLL + u
                count = used[r]
                lhs = jnp.concatenate([tiles[r, t] for t in range(TPR)], axis=1)
                rhs = jnp.concatenate(
                    [labels[jnp.where(t < count, col[t, r], RB + HB)] for t in range(TPR)], axis=0
                )
                mixed = jnp.dot(lhs, rhs, preferred_element_type=F32)
                current = PROPAGATE * mixed + (1.0 - PROPAGATE) * seed[r].astype(F32)
                wide[pl.ds(pl.multiple_of(r * B, B), B), :] = current
                if following is not None:
                    following[pl.ds(r, 1)] = current.astype(BF16)[None]
            return carry

        lax.fori_loop(0, RB // UNROLL, several, 0)

    def unpack(received, labels):
        def several(h, carry):
            x = received[pl.ds(h * (B // SLOT), B // SLOT)].astype(F32)
            left = lax.broadcasted_iota(jnp.int32, x.shape, 2) < HALF // 2
            first = jnp.where(left, x, 0.0)
            second = jnp.where(left, pltpu.roll(x, HALF // 2, 2), 0.0)
            both = jnp.concatenate([first, second], axis=1).astype(BF16)
            labels[pl.ds(RB + h, 1)] = both.reshape(1, B, HALF)
            return carry

        lax.fori_loop(0, HB, several, 0, unroll=4)

    multiply(seed_a, seed_a, one_a, wide_a)
    put_own(one_a, rows_a(me))
    sent_a1 = spread(rows_a, send_a1, own_place(one_a), 1)
    multiply(seed_b, seed_b, one_b, wide_b)
    recv_b1[pl.ds(me, 1)] = rows_b(me)[None]
    sent_b1 = spread(rows_b, send_b1, recv_b1.at[me], 2)

    sent_a1.wait_recv()
    multiply(one_a, seed_a, two_a, wide_a)
    put_own(two_a, rows_a(me))
    sent_a2 = spread(rows_a, send_a2, own_place(two_a), 3)
    sent_b1.wait_recv()
    unpack(recv_b1, one_b)
    multiply(one_b, seed_b, two_b, wide_b)
    recv_b2[pl.ds(me, 1)] = rows_b(me)[None]
    sent_b2 = spread(rows_b, send_b2, recv_b2.at[me], 4)

    sent_a2.wait_recv()
    multiply(two_a, seed_a, None, wide_a)
    sent_b2.wait_recv()
    unpack(recv_b2, two_b)
    multiply(two_b, seed_b, None, wide_b)
    for sent in (near, far, features_sent, sent_a1, sent_b1, sent_a2, sent_b2):
        sent.wait_send()


def propagate(rows_t, counts, features, wt, bias, ema, target, tiles, cols_t, used):
    wide = jax.ShapeDtypeStruct((ROWS, HALF), F32)
    labels = pltpu.VMEM((RB + HB + 1, B, HALF), BF16)
    slots = pltpu.VMEM((N, SLOT, HALF), BF16)
    small = pltpu.VMEM((N, PACK, HALF), BF16)
    row = pltpu.VMEM((1, CP), F32)
    vector = pltpu.VMEM((1, C), F32)
    return pl.pallas_call(
        propagate_kernel,
        out_shape=(wide, wide),
        in_specs=[in_hbm()] * 10,
        out_specs=(in_vmem(), in_vmem()),
        scratch_shapes=[
            pltpu.VMEM((SLOT, N), jnp.int32),
            pltpu.VMEM((N, B), jnp.int32),
            pltpu.SMEM((N, B), jnp.int32),
            pltpu.SMEM((N,), jnp.int32),
            pltpu.VMEM((ROWS, F), BF16),
            pltpu.VMEM((C, F), BF16),
            vector, vector, vector,
            pltpu.VMEM((RB, TPR, B, B), BF16),
            pltpu.SMEM((TPR, RB), jnp.int32),
            pltpu.SMEM((RB,), jnp.int32),
            pltpu.VMEM((CP, F), F32),
            row, row, row,
            pltpu.VMEM((SLOT, HALF), F32),
            labels, labels, labels, labels, labels, labels,
            slots, slots, slots, slots, small, small, small, small,
            pltpu.VMEM((GROUP, 8, CP), F32),
            pltpu.VMEM((N // GROUP, 8, CP), F32),
            pltpu.SemaphoreType.DMA((10,)),
            pltpu.SemaphoreType.DMA,
            pltpu.SemaphoreType.DMA((7,)),
            pltpu.SemaphoreType.DMA((7,)),
        ],
        compiler_params=pltpu.CompilerParams(collective_id=0, has_side_effects=True, vmem_limit_bytes=VMEM_LIMIT),
        cost_estimate=pl.CostEstimate(
            flops=6 * RB * TPR * B * B * CP, bytes_accessed=24 * 2**20, transcendentals=(ROWS + HB * B) * CP
        ),
        name="propagate",
    )(rows_t, counts, features, wt, bias, ema, target, tiles, cols_t, used)


LOG_ROWS = 1024


def log_kernel(a_ref, b_ref, out_ref):
    for i in range(LOG_ROWS // B):
        a = a_ref[pl.ds(i * B, B), :].T
        b = b_ref[pl.ds(i * B, B), :].T
        out_ref[pl.ds(0, HALF), pl.ds(i * B, B)] = jnp.log(a + LOG_FLOOR)
        out_ref[pl.ds(HALF, C - HALF), pl.ds(i * B, B)] = jnp.log(b[: C - HALF] + LOG_FLOOR)


def log_scores(a, b):
    part = pl.BlockSpec((LOG_ROWS, HALF), lambda i: (i, 0))
    return pl.pallas_call(
        log_kernel,
        grid=(ROWS // LOG_ROWS,),
        out_shape=jax.ShapeDtypeStruct((C, ROWS), F32),
        in_specs=[part, part],
        out_specs=pl.BlockSpec((C, LOG_ROWS), lambda i: (0, i)),
        compiler_params=pltpu.CompilerParams(vmem_limit_bytes=VMEM_LIMIT),
        cost_estimate=pl.CostEstimate(flops=0, bytes_accessed=14 * 2**20, transcendentals=ROWS * C),
        name="log_scores",
    )(a, b)


def on_device(
    features, teacher_w, teacher_b, ema_prior, target_prior, send_rows, send_count, tiles, tile_col, tile_count
):
    a, b = propagate(
        send_rows.T, send_count, features, teacher_w.T, teacher_b.reshape(1, C), ema_prior.reshape(1, C),
        target_prior.reshape(1, C), tiles, tile_col.T, tile_count,
    )
    return log_scores(a, b).T


def solution(mesh):
    placed = (
        P("dom", None), P(), P(), P(), P(), P("dom", None), P("dom"),
        P("dom", None, None, None), P("dom", None), P("dom"),
    )
    return jax.shard_map(on_device, mesh=mesh, in_specs=placed, out_specs=P("dom", None), check_vma=False)
```

```python
import jax
import jax.numpy as jnp
from jax import lax
from jax.experimental import pallas as pl
from jax.experimental.pallas import tpu as pltpu
from jax.sharding import PartitionSpec as P

F = 128
C = 172
CP = 256
B = 128
RB = 64
TPR = 8
SLOT = 32
HALF = 128
PACK = 16
CHUNK = 1024
UNROLL = 8
HB = 32
ROWS = 8192
N = 128
NODES = ROWS * N

MOMENTUM = 0.7
PROPAGATE = 0.9
LOG_FLOOR = 0.0001
DEAD = 32768.0
LOW = -1e30
VMEM_LIMIT = 58 * 2**20
GANG = 8
MESH = pl.DeviceIdType.MESH
MIX = 37
GROUP = 16
F32 = jnp.float32
BF16 = jnp.bfloat16


def in_hbm():
    return pl.BlockSpec(memory_space=pltpu.HBM)


def in_vmem():
    return pl.BlockSpec(memory_space=pltpu.VMEM)


def propagate_kernel(
    rows_hbm, cnt_hbm, feat_hbm, wt_hbm, b_hbm, ema_hbm, target_hbm, tiles_hbm, col_hbm, used_hbm,
    out_ref,
    wide_a, wide_b, rows_v, rows_w, rows, cnt, feat, wt, bias, ema, target, tiles, col, used,
    wpad, bpad, epad, tpad,
    seed_a, seed_b, one_a, one_b, two_a, two_b,
    send_a, send_b, feat_recv, recv_b1, recv_b2,
    part1, part2, load_sem, flip_sem, send_sem, recv_sem,
):
    me = lax.axis_index("dom")
    next_door = lax.rem(me + 1, N)

    loads = [
        pltpu.make_async_copy(src, dst, load_sem.at[i])
        for i, (src, dst) in enumerate(
            (
                (rows_hbm, rows_v), (feat_hbm, feat), (cnt_hbm, cnt), (wt_hbm, wt), (b_hbm, bias), (ema_hbm, ema),
                (target_hbm, target), (col_hbm, col), (used_hbm, used), (tiles_hbm, tiles),
            )
        )
    ]
    for load in loads[:9]:
        load.start()

    barrier = pltpu.get_barrier_semaphore()

    def tell(k, carry):
        pl.semaphore_signal(barrier, inc=1, device_id=(lax.rem(me + k, N),), device_id_type=MESH)
        return carry

    lax.fori_loop(1, N, tell, 0)

    loads[0].wait()
    rows_w[...] = jnp.concatenate([rows_v[...], jnp.zeros((B - SLOT, N), jnp.int32)], axis=0).T
    flip = pltpu.make_async_copy(rows_w, rows, flip_sem)
    flip.start()
    loads[1].wait()

    def widen(k, carry):
        at = pl.multiple_of(k * CHUNK, CHUNK)
        wide_a[pl.ds(at, CHUNK), :] = feat[pl.ds(at, CHUNK), :].astype(F32)
        return carry

    lax.fori_loop(0, ROWS // CHUNK, widen, 0)
    for load in loads[2:9]:
        load.wait()
    flip.wait()

    def picked(wide, dest, dead):
        taken = jnp.concatenate([wide[pl.ds(rows[dest, j], 1), :] for j in range(SLOT)], axis=0)
        live = lax.broadcasted_iota(jnp.int32, (SLOT, HALF), 0) < cnt[dest]
        return jnp.where(live, taken, dead)

    def packed(values):
        lane = lax.broadcasted_iota(jnp.int32, (PACK, HALF), 1)
        return jnp.where(lane < HALF // 2, values[:PACK], pltpu.roll(values[PACK:], HALF // 2, 1))

    def spread(make, sendbuf, landing, number, first=0, last=N):
        def gang(base, turns):
            dests = [lax.rem(me + lax.rem((base + u) * MIX, N), N) for u in turns]
            for u, dest in zip(turns, dests):
                sendbuf[pl.ds(base + u, 1)] = make(dest)[None]
            for u, dest in zip(turns, dests):
                pltpu.make_async_remote_copy(
                    src_ref=sendbuf.at[base + u], dst_ref=landing(base + u),
                    send_sem=send_sem.at[number], recv_sem=recv_sem.at[number],
                    device_id=(dest,), device_id_type=MESH,
                ).start()

        def several(i, carry):
            gang(i * GANG, range(GANG))
            return carry

        if first == 0:
            gang(0, range(1, GANG))
        lax.fori_loop(max(first // GANG, 1), last // GANG, several, 0)
        whole = sendbuf.at[pl.ds(0, last - max(first, 1))]
        return pltpu.make_async_remote_copy(
            src_ref=whole, dst_ref=whole, send_sem=send_sem.at[number], recv_sem=recv_sem.at[number],
            device_id=(next_door,), device_id_type=MESH,
        )

    block_me = RB + me // (B // SLOT)
    row_me = pl.multiple_of(lax.rem(me, B // SLOT) * SLOT, SLOT)

    def own_place(labels):
        return lambda turn: labels.at[block_me, pl.ds(row_me, SLOT), :]

    def put_own(labels, values):
        labels[pl.ds(block_me, 1), pl.ds(row_me, SLOT), :] = values[None]

    def feature_rows(dest):
        return picked(wide_a, dest, DEAD).astype(BF16)

    def rows_a(dest):
        return picked(wide_a, dest, 0.0).astype(BF16)

    def rows_b(dest):
        return packed(picked(wide_b, dest, 0.0)).astype(BF16)

    wpad[...] = jnp.zeros_like(wpad)
    wpad[pl.ds(0, C), :] = wt[...].astype(F32)
    bpad[...] = jnp.full(bpad.shape, LOW, F32)
    bpad[:, pl.ds(0, C)] = bias[...]
    epad[...] = jnp.full(epad.shape, 1.0, F32)
    epad[:, pl.ds(0, C)] = ema[...]
    tpad[...] = jnp.zeros_like(tpad)
    tpad[:, pl.ds(0, C)] = target[...]
    weights = wpad[...].astype(BF16)
    blocks = CHUNK // B

    def soft(values):
        logits = lax.dot_general(values, weights, (((1,), (1,)), ((), ())), preferred_element_type=F32) + bpad[...]
        e = jnp.exp(logits - jnp.max(logits, axis=-1, keepdims=True))
        return e * (1.0 / jnp.sum(e, axis=-1, keepdims=True))

    def local(k, acc):
        p = soft(feat[pl.ds(pl.multiple_of(k * CHUNK, CHUNK), CHUNK), :]).astype(BF16)
        seed_a[pl.ds(k * blocks, blocks)] = p[:, :HALF].reshape(blocks, B, HALF)
        seed_b[pl.ds(k * blocks, blocks)] = p[:, HALF:].reshape(blocks, B, HALF)
        return acc + jnp.sum(p.astype(F32).reshape(CHUNK // 8, 8, CP), axis=0)

    acc = lax.fori_loop(0, ROWS // CHUNK, local, jnp.zeros((8, CP), F32))
    pl.semaphore_wait(barrier, N - 1)

    group = me // GROUP
    place = lax.rem(me, GROUP)
    groups = N // GROUP
    part1[pl.ds(place, 1)] = acc[None]

    def send_near(k, carry):
        pltpu.make_async_remote_copy(
            src_ref=part1.at[place], dst_ref=part1.at[place], send_sem=send_sem.at[5], recv_sem=recv_sem.at[5],
            device_id=(group * GROUP + lax.rem(place + k, GROUP),), device_id_type=MESH,
        ).start()
        return carry

    lax.fori_loop(1, GROUP, send_near, 0)
    near = pltpu.make_async_remote_copy(
        src_ref=part1.at[pl.ds(0, GROUP - 1)], dst_ref=part1.at[pl.ds(0, GROUP - 1)],
        send_sem=send_sem.at[5], recv_sem=recv_sem.at[5], device_id=(next_door,), device_id_type=MESH,
    )

    def landing(turn):
        return feat_recv.at[turn]

    feat_recv[pl.ds(0, 1)] = feature_rows(me)[None]
    early = spread(feature_rows, send_a, landing, 0, 0, N // 2)
    near.wait_recv()
    part2[pl.ds(group, 1)] = jnp.sum(part1[...], axis=0)[None]

    def send_far(k, carry):
        pltpu.make_async_remote_copy(
            src_ref=part2.at[group], dst_ref=part2.at[group], send_sem=send_sem.at[6], recv_sem=recv_sem.at[6],
            device_id=(lax.rem(group + k, groups) * GROUP + place,), device_id_type=MESH,
        ).start()
        return carry

    lax.fori_loop(1, groups, send_far, 0)
    far = pltpu.make_async_remote_copy(
        src_ref=part2.at[pl.ds(0, groups - 1)], dst_ref=part2.at[pl.ds(0, groups - 1)],
        send_sem=send_sem.at[6], recv_sem=recv_sem.at[6], device_id=(next_door,), device_id_type=MESH,
    )
    late = spread(feature_rows, send_a, landing, 7, N // 2, N)
    loads[9].start()
    for labels in (seed_a, seed_b, one_a, one_b, two_a, two_b):
        labels[pl.ds(RB + HB, 1)] = jnp.zeros((1, B, HALF), BF16)

    far.wait_recv()
    total = jnp.sum(jnp.sum(part2[...], axis=0), axis=0, keepdims=True)
    ratio = tpad[...] / (MOMENTUM * epad[...] + (1.0 - MOMENTUM) * total / NODES)

    def aligned(p_a, p_b):
        a = p_a.astype(F32) * ratio[:, :HALF]
        b = p_b.astype(F32) * ratio[:, HALF:]
        row_total = jnp.sum(a + b, axis=-1, keepdims=True)
        scale = 1.0 / jnp.where(row_total > 0.0, row_total, 1.0)
        return (a * scale).astype(BF16), (b * scale).astype(BF16)

    def align(k, carry):
        a, b = aligned(
            seed_a[pl.ds(k * blocks, blocks)].reshape(CHUNK, HALF), seed_b[pl.ds(k * blocks, blocks)].reshape(CHUNK, HALF)
        )
        seed_a[pl.ds(k * blocks, blocks)] = a.reshape(blocks, B, HALF)
        seed_b[pl.ds(k * blocks, blocks)] = b.reshape(blocks, B, HALF)
        return carry

    lax.fori_loop(0, RB * B // CHUNK, align, 0)

    sources = CHUNK // SLOT

    def boundary(k, carry):
        f = feat_recv[pl.ds(k * sources, sources)].reshape(CHUNK, F)
        live = f[:, :1].astype(F32) < DEAD / 2
        p = jnp.where(live, soft(f), 0.0).astype(BF16)
        a, b = aligned(p[:, :HALF], p[:, HALF:])
        for u in range(sources):
            source = lax.rem(me + N - lax.rem((k * sources + u) * MIX, N), N)
            block = RB + source // (B // SLOT)
            row = pl.multiple_of(lax.rem(source, B // SLOT) * SLOT, SLOT)
            seed_a[pl.ds(block, 1), pl.ds(row, SLOT), :] = a[u * SLOT : (u + 1) * SLOT][None]
            seed_b[pl.ds(block, 1), pl.ds(row, SLOT), :] = b[u * SLOT : (u + 1) * SLOT][None]
        return carry

    turns = N // sources
    early.wait_recv()
    lax.fori_loop(0, turns // 2, boundary, 0)
    late.wait_recv()
    lax.fori_loop(turns // 2, turns, boundary, 0)
    loads[9].wait()

    def multiply(labels, seeds, following, wides):
        def several(i, carry):
            for u in range(UNROLL):
                r = i * UNROLL + u
                count = used[r]
                lhs = jnp.concatenate([tiles[r, t] for t in range(TPR)], axis=1)
                cols = [jnp.where(t < count, col[t, r], RB + HB) for t in range(TPR)]
                rhs = jnp.concatenate([jnp.concatenate([part[c] for part in labels], axis=1) for c in cols], axis=0)
                mixed = jnp.dot(lhs, rhs, preferred_element_type=F32)
                for q, seed in enumerate(seeds):
                    own = mixed[:, q * HALF : (q + 1) * HALF]
                    current = PROPAGATE * own + (1.0 - PROPAGATE) * seed[r].astype(F32)
                    at = pl.multiple_of(r * B, B)
                    if following:
                        wides[q][pl.ds(at, B), :] = current
                        following[q][pl.ds(r, 1)] = current.astype(BF16)[None]
                    else:
                        low, high = q * HALF, min((q + 1) * HALF, C)
                        out_ref[pl.ds(low, high - low), pl.ds(at, B)] = jnp.log(current.T[: high - low] + LOG_FLOOR)
            return carry

        lax.fori_loop(0, RB // UNROLL, several, 0)

    def unpack(received, labels):
        def several(h, carry):
            x = received[pl.ds(h * (B // SLOT), B // SLOT)].astype(F32)
            left = lax.broadcasted_iota(jnp.int32, x.shape, 2) < HALF // 2
            first = jnp.where(left, x, 0.0)
            second = jnp.where(left, pltpu.roll(x, HALF // 2, 2), 0.0)
            both = jnp.concatenate([first, second], axis=1).astype(BF16)
            labels[pl.ds(RB + h, 1)] = both.reshape(1, B, HALF)
            return carry

        lax.fori_loop(0, HB, several, 0, unroll=4)

    def here(received):
        return lambda turn: received.at[me]

    multiply((seed_a, seed_b), (seed_a, seed_b), (one_a, one_b), (wide_a, wide_b))
    early.wait_send()
    late.wait_send()
    put_own(one_a, rows_a(me))
    sent_a1 = spread(rows_a, send_a, own_place(one_a), 1)
    recv_b1[pl.ds(me, 1)] = rows_b(me)[None]
    sent_b1 = spread(rows_b, send_b, here(recv_b1), 2)

    sent_a1.wait_recv()
    multiply((one_a,), (seed_a,), (two_a,), (wide_a,))
    sent_a1.wait_send()
    put_own(two_a, rows_a(me))
    sent_a2 = spread(rows_a, send_a, own_place(two_a), 3)
    sent_b1.wait_recv()
    unpack(recv_b1, one_b)
    multiply((one_b,), (seed_b,), (two_b,), (wide_b,))
    sent_b1.wait_send()
    recv_b2[pl.ds(me, 1)] = rows_b(me)[None]
    sent_b2 = spread(rows_b, send_b, here(recv_b2), 4)

    sent_a2.wait_recv()
    sent_b2.wait_recv()
    unpack(recv_b2, two_b)
    multiply((two_a, two_b), (seed_a, seed_b), (), ())
    for sent in (near, far, sent_a2, sent_b2):
        sent.wait_send()


def propagate(rows_t, counts, features, wt, bias, ema, target, tiles, cols_t, used):
    wide = pltpu.VMEM((ROWS, HALF), F32)
    labels = pltpu.VMEM((RB + HB + 1, B, HALF), BF16)
    slots = pltpu.VMEM((N, SLOT, HALF), BF16)
    small = pltpu.VMEM((N, PACK, HALF), BF16)
    row = pltpu.VMEM((1, CP), F32)
    vector = pltpu.VMEM((1, C), F32)
    return pl.pallas_call(
        propagate_kernel,
        out_shape=jax.ShapeDtypeStruct((C, ROWS), F32),
        in_specs=[in_hbm()] * 10,
        out_specs=in_vmem(),
        scratch_shapes=[
            wide, wide,
            pltpu.VMEM((SLOT, N), jnp.int32),
            pltpu.VMEM((N, B), jnp.int32),
            pltpu.SMEM((N, B), jnp.int32),
            pltpu.SMEM((N,), jnp.int32),
            pltpu.VMEM((ROWS, F), BF16),
            pltpu.VMEM((C, F), BF16),
            vector, vector, vector,
            pltpu.VMEM((RB, TPR, B, B), BF16),
            pltpu.SMEM((TPR, RB), jnp.int32),
            pltpu.SMEM((RB,), jnp.int32),
            pltpu.VMEM((CP, F), F32),
            row, row, row,
            labels, labels, labels, labels, labels, labels,
            slots, small, slots, small, small,
            pltpu.VMEM((GROUP, 8, CP), F32),
            pltpu.VMEM((N // GROUP, 8, CP), F32),
            pltpu.SemaphoreType.DMA((10,)),
            pltpu.SemaphoreType.DMA,
            pltpu.SemaphoreType.DMA((8,)),
            pltpu.SemaphoreType.DMA((8,)),
        ],
        compiler_params=pltpu.CompilerParams(collective_id=0, has_side_effects=True, vmem_limit_bytes=VMEM_LIMIT),
        cost_estimate=pl.CostEstimate(
            flops=6 * RB * TPR * B * B * CP, bytes_accessed=24 * 2**20, transcendentals=(ROWS + HB * B) * CP
        ),
        name="propagate",
    )(rows_t, counts, features, wt, bias, ema, target, tiles, cols_t, used)


def on_device(
    features, teacher_w, teacher_b, ema_prior, target_prior, send_rows, send_count, tiles, tile_col, tile_count
):
    out_t = propagate(
        send_rows.T, send_count, features, teacher_w.T, teacher_b.reshape(1, C), ema_prior.reshape(1, C),
        target_prior.reshape(1, C), tiles, tile_col.T, tile_count,
    )
    return out_t.T


def solution(mesh):
    placed = (
        P("dom", None), P(), P(), P(), P(), P("dom", None), P("dom"),
        P("dom", None, None, None), P("dom", None), P("dom"),
    )
    return jax.shard_map(on_device, mesh=mesh, in_specs=placed, out_specs=P("dom", None), check_vma=False)
```

```python
import jax
import jax.numpy as jnp
from jax import lax
from jax.experimental import pallas as pl
from jax.experimental.pallas import tpu as pltpu
from jax.sharding import PartitionSpec as P

F = 128
C = 172
CP = 256
B = 128
RB = 64
TPR = 8
SLOT = 32
HALF = 128
PACK = 16
CHUNK = 1024
UNROLL = 8
HB = 32
ROWS = 8192
N = 128
NODES = ROWS * N

MOMENTUM = 0.7
PROPAGATE = 0.9
LOG_FLOOR = 0.0001
DEAD = 32768.0
LOW = -1e30
VMEM_LIMIT = 50 * 2**20
GANG = 8
MESH = pl.DeviceIdType.MESH
MIX = 37
GROUP = 16
F32 = jnp.float32
BF16 = jnp.bfloat16


def in_hbm():
    return pl.BlockSpec(memory_space=pltpu.HBM)


def in_vmem():
    return pl.BlockSpec(memory_space=pltpu.VMEM)


def propagate_kernel(
    rows_hbm, cnt_hbm, feat_hbm, wt_hbm, b_hbm, ema_hbm, target_hbm, tiles_hbm, col_hbm, used_hbm,
    out_ref,
    wide_a, wide_b, rows_v, rows_w, rows, cnt, feat, wt, bias, ema, target, tiles, col, used,
    wpad, bpad, epad, tpad,
    seed_a, seed_b, one_a, one_b, two_a, two_b,
    send_a, send_b, feat_recv, recv_b1, recv_b2,
    part1, part2, load_sem, flip_sem, send_sem, recv_sem,
):
    me = lax.axis_index("dom")
    next_door = lax.rem(me + 1, N)

    loads = [
        pltpu.make_async_copy(src, dst, load_sem.at[i])
        for i, (src, dst) in enumerate(
            (
                (rows_hbm, rows_v), (feat_hbm, feat), (cnt_hbm, cnt), (wt_hbm, wt), (b_hbm, bias), (ema_hbm, ema),
                (target_hbm, target), (col_hbm, col), (used_hbm, used), (tiles_hbm, tiles),
            )
        )
    ]
    for load in loads[:9]:
        load.start()

    barrier = pltpu.get_barrier_semaphore()

    def tell(k, carry):
        pl.semaphore_signal(barrier, inc=1, device_id=(lax.rem(me + k, N),), device_id_type=MESH)
        return carry

    lax.fori_loop(1, N, tell, 0)

    loads[0].wait()
    rows_w[...] = jnp.concatenate([rows_v[...], jnp.zeros((B - SLOT, N), jnp.int32)], axis=0).T
    flip = pltpu.make_async_copy(rows_w, rows, flip_sem)
    flip.start()
    loads[1].wait()

    def widen(k, carry):
        at = pl.multiple_of(k * CHUNK, CHUNK)
        wide_a[pl.ds(at, CHUNK), :] = feat[pl.ds(at, CHUNK), :].astype(F32)
        return carry

    lax.fori_loop(0, ROWS // CHUNK, widen, 0)
    for load in loads[2:9]:
        load.wait()
    flip.wait()

    def picked(wide, dest, dead):
        taken = jnp.concatenate([wide[pl.ds(rows[dest, j], 1), :] for j in range(SLOT)], axis=0)
        live = lax.broadcasted_iota(jnp.int32, (SLOT, HALF), 0) < cnt[dest]
        return jnp.where(live, taken, dead)

    def packed(values):
        lane = lax.broadcasted_iota(jnp.int32, (PACK, HALF), 1)
        return jnp.where(lane < HALF // 2, values[:PACK], pltpu.roll(values[PACK:], HALF // 2, 1))

    def turned(turn, sign):
        return lax.rem(me + N + sign * lax.rem((turn + 1) * MIX, N), N)

    def spread(make, sendbuf, landing, number, first=0, last=N):
        def gang(base, size):
            dests = [turned(base + u, 1) for u in range(size)]
            for u, dest in enumerate(dests):
                sendbuf[pl.ds(base + u, 1)] = make(dest)[None]
            for u, dest in enumerate(dests):
                pltpu.make_async_remote_copy(
                    src_ref=sendbuf.at[base + u], dst_ref=landing(base + u),
                    send_sem=send_sem.at[number], recv_sem=recv_sem.at[number],
                    device_id=(dest,), device_id_type=MESH,
                ).start()

        def several(i, carry):
            gang(i * GANG, GANG)
            return carry

        full = last // GANG - (last == N)
        lax.fori_loop(first // GANG, full, several, 0)
        if last == N:
            gang(full * GANG, GANG - 1)
        whole = sendbuf.at[pl.ds(0, last - first - (last == N))]
        return pltpu.make_async_remote_copy(
            src_ref=whole, dst_ref=whole, send_sem=send_sem.at[number], recv_sem=recv_sem.at[number],
            device_id=(next_door,), device_id_type=MESH,
        )

    block_me = RB + me // (B // SLOT)
    row_me = pl.multiple_of(lax.rem(me, B // SLOT) * SLOT, SLOT)

    def own_place(labels):
        return lambda turn: labels.at[block_me, pl.ds(row_me, SLOT), :]

    def put_own(labels, values):
        labels[pl.ds(block_me, 1), pl.ds(row_me, SLOT), :] = values[None]

    def feature_rows(dest):
        return picked(wide_a, dest, DEAD).astype(BF16)

    def rows_a(dest):
        return picked(wide_a, dest, 0.0).astype(BF16)

    def rows_b(dest):
        return packed(picked(wide_b, dest, 0.0)).astype(BF16)

    def landing(turn):
        return feat_recv.at[turn]

    feat_recv[pl.ds(N - 1, 1)] = feature_rows(me)[None]
    pl.semaphore_wait(barrier, N - 1)
    early = spread(feature_rows, send_a, landing, 0, 0, N // 2)
    late = spread(feature_rows, send_a, landing, 7, N // 2, N)
    loads[9].start()

    wpad[...] = jnp.zeros_like(wpad)
    wpad[pl.ds(0, C), :] = wt[...].astype(F32)
    bpad[...] = jnp.full(bpad.shape, LOW, F32)
    bpad[:, pl.ds(0, C)] = bias[...]
    epad[...] = jnp.full(epad.shape, 1.0, F32)
    epad[:, pl.ds(0, C)] = ema[...]
    tpad[...] = jnp.zeros_like(tpad)
    tpad[:, pl.ds(0, C)] = target[...]
    weights = wpad[...].astype(BF16)
    blocks = CHUNK // B

    def soft(values):
        logits = lax.dot_general(values, weights, (((1,), (1,)), ((), ())), preferred_element_type=F32) + bpad[...]
        e = jnp.exp(logits - jnp.max(logits, axis=-1, keepdims=True))
        return e * (1.0 / jnp.sum(e, axis=-1, keepdims=True))

    def local(k, acc):
        p = soft(feat[pl.ds(pl.multiple_of(k * CHUNK, CHUNK), CHUNK), :]).astype(BF16)
        seed_a[pl.ds(k * blocks, blocks)] = p[:, :HALF].reshape(blocks, B, HALF)
        seed_b[pl.ds(k * blocks, blocks)] = p[:, HALF:].reshape(blocks, B, HALF)
        return acc + jnp.sum(p.astype(F32).reshape(CHUNK // 8, 8, CP), axis=0)

    acc = lax.fori_loop(0, ROWS // CHUNK, local, jnp.zeros((8, CP), F32))

    group = me // GROUP
    place = lax.rem(me, GROUP)
    groups = N // GROUP
    part1[pl.ds(place, 1)] = acc[None]

    def send_near(k, carry):
        pltpu.make_async_remote_copy(
            src_ref=part1.at[place], dst_ref=part1.at[place], send_sem=send_sem.at[5], recv_sem=recv_sem.at[5],
            device_id=(group * GROUP + lax.rem(place + k, GROUP),), device_id_type=MESH,
        ).start()
        return carry

    lax.fori_loop(1, GROUP, send_near, 0)
    near = pltpu.make_async_remote_copy(
        src_ref=part1.at[pl.ds(0, GROUP - 1)], dst_ref=part1.at[pl.ds(0, GROUP - 1)],
        send_sem=send_sem.at[5], recv_sem=recv_sem.at[5], device_id=(next_door,), device_id_type=MESH,
    )

    sources = CHUNK // SLOT

    def boundary(k, carry):
        f = feat_recv[pl.ds(k * sources, sources)].reshape(CHUNK, F)
        live = f[:, :1].astype(F32) < DEAD / 2
        p = jnp.where(live, soft(f), 0.0).astype(BF16)
        for u in range(sources):
            source = turned(k * sources + u, -1)
            block = RB + source // (B // SLOT)
            row = pl.multiple_of(lax.rem(source, B // SLOT) * SLOT, SLOT)
            seed_a[pl.ds(block, 1), pl.ds(row, SLOT), :] = p[u * SLOT : (u + 1) * SLOT, :HALF][None]
            seed_b[pl.ds(block, 1), pl.ds(row, SLOT), :] = p[u * SLOT : (u + 1) * SLOT, HALF:][None]
        return carry

    turns = N // sources
    for labels in (seed_a, seed_b, one_a, one_b, two_a, two_b):
        labels[pl.ds(RB + HB, 1)] = jnp.zeros((1, B, HALF), BF16)
    early.wait_recv()
    lax.fori_loop(0, turns // 2, boundary, 0)
    near.wait_recv()
    part2[pl.ds(group, 1)] = jnp.sum(part1[...], axis=0)[None]

    def send_far(k, carry):
        pltpu.make_async_remote_copy(
            src_ref=part2.at[group], dst_ref=part2.at[group], send_sem=send_sem.at[6], recv_sem=recv_sem.at[6],
            device_id=(lax.rem(group + k, groups) * GROUP + place,), device_id_type=MESH,
        ).start()
        return carry

    lax.fori_loop(1, groups, send_far, 0)
    far = pltpu.make_async_remote_copy(
        src_ref=part2.at[pl.ds(0, groups - 1)], dst_ref=part2.at[pl.ds(0, groups - 1)],
        send_sem=send_sem.at[6], recv_sem=recv_sem.at[6], device_id=(next_door,), device_id_type=MESH,
    )
    late.wait_recv()
    lax.fori_loop(turns // 2, turns, boundary, 0)
    far.wait_recv()
    total = jnp.sum(jnp.sum(part2[...], axis=0), axis=0, keepdims=True)
    ratio = tpad[...] / (MOMENTUM * epad[...] + (1.0 - MOMENTUM) * total / NODES)

    def aligned(p_a, p_b):
        a = p_a.astype(F32) * ratio[:, :HALF]
        b = p_b.astype(F32) * ratio[:, HALF:]
        row_total = jnp.sum(a + b, axis=-1, keepdims=True)
        scale = 1.0 / jnp.where(row_total > 0.0, row_total, 1.0)
        return (a * scale).astype(BF16), (b * scale).astype(BF16)

    def align(k, carry):
        a, b = aligned(
            seed_a[pl.ds(k * blocks, blocks)].reshape(CHUNK, HALF), seed_b[pl.ds(k * blocks, blocks)].reshape(CHUNK, HALF)
        )
        seed_a[pl.ds(k * blocks, blocks)] = a.reshape(blocks, B, HALF)
        seed_b[pl.ds(k * blocks, blocks)] = b.reshape(blocks, B, HALF)
        return carry

    lax.fori_loop(0, (RB + HB) * B // CHUNK, align, 0)
    loads[9].wait()

    def multiply(labels, seeds, following, wides, low=None):
        def several(i, carry):
            for u in range(UNROLL):
                r = i * UNROLL + u
                count = used[r]
                lhs = jnp.concatenate([tiles[r, t] for t in range(TPR)], axis=1)
                cols = [jnp.where(t < count, col[t, r], RB + HB) for t in range(TPR)]
                rhs = jnp.concatenate([jnp.concatenate([part[c] for part in labels], axis=1) for c in cols], axis=0)
                mixed = jnp.dot(lhs, rhs, preferred_element_type=F32)
                for q, seed in enumerate(seeds):
                    own = mixed[:, q * HALF : (q + 1) * HALF]
                    current = PROPAGATE * own + (1.0 - PROPAGATE) * seed[r].astype(F32)
                    at = pl.multiple_of(r * B, B)
                    if following:
                        wides[q][pl.ds(at, B), :] = current
                        following[q][pl.ds(r, 1)] = current.astype(BF16)[None]
                    else:
                        classes = min(HALF, C - low)
                        out_ref[pl.ds(low, classes), pl.ds(at, B)] = jnp.log(current.T[:classes] + LOG_FLOOR)
            return carry

        lax.fori_loop(0, RB // UNROLL, several, 0)

    def unpack(received, labels):
        def several(h, carry):
            x = received[pl.ds(h * (B // SLOT), B // SLOT)].astype(F32)
            left = lax.broadcasted_iota(jnp.int32, x.shape, 2) < HALF // 2
            first = jnp.where(left, x, 0.0)
            second = jnp.where(left, pltpu.roll(x, HALF // 2, 2), 0.0)
            both = jnp.concatenate([first, second], axis=1).astype(BF16)
            labels[pl.ds(RB + h, 1)] = both.reshape(1, B, HALF)
            return carry

        lax.fori_loop(0, HB, several, 0, unroll=4)

    def here(received):
        return lambda turn: received.at[me]

    multiply((seed_a, seed_b), (seed_a, seed_b), (one_a, one_b), (wide_a, wide_b))
    early.wait_send()
    late.wait_send()
    recv_b1[pl.ds(me, 1)] = rows_b(me)[None]
    sent_b1 = spread(rows_b, send_b, here(recv_b1), 2)
    put_own(one_a, rows_a(me))
    sent_a1 = spread(rows_a, send_a, own_place(one_a), 1)

    sent_b1.wait_recv()
    unpack(recv_b1, one_b)
    multiply((one_b,), (seed_b,), (two_b,), (wide_b,))
    sent_b1.wait_send()
    recv_b2[pl.ds(me, 1)] = rows_b(me)[None]
    sent_b2 = spread(rows_b, send_b, here(recv_b2), 4)
    sent_a1.wait_recv()
    multiply((one_a,), (seed_a,), (two_a,), (wide_a,))
    sent_a1.wait_send()
    put_own(two_a, rows_a(me))
    sent_a2 = spread(rows_a, send_a, own_place(two_a), 3)

    sent_b2.wait_recv()
    unpack(recv_b2, two_b)
    multiply((two_b,), (seed_b,), (), (), HALF)
    sent_a2.wait_recv()
    multiply((two_a,), (seed_a,), (), (), 0)
    for sent in (near, far, sent_b2, sent_a2):
        sent.wait_send()


def propagate(rows_t, counts, features, wt, bias, ema, target, tiles, cols_t, used):
    wide = pltpu.VMEM((ROWS, HALF), F32)
    labels = pltpu.VMEM((RB + HB + 1, B, HALF), BF16)
    slots = pltpu.VMEM((N, SLOT, HALF), BF16)
    small = pltpu.VMEM((N, PACK, HALF), BF16)
    row = pltpu.VMEM((1, CP), F32)
    vector = pltpu.VMEM((1, C), F32)
    return pl.pallas_call(
        propagate_kernel,
        out_shape=pltpu.VMEM((C, ROWS), F32),
        in_specs=[in_hbm()] * 10,
        out_specs=in_vmem(),
        scratch_shapes=[
            wide, wide,
            pltpu.VMEM((SLOT, N), jnp.int32),
            pltpu.VMEM((N, B), jnp.int32),
            pltpu.SMEM((N, B), jnp.int32),
            pltpu.SMEM((N,), jnp.int32),
            pltpu.VMEM((ROWS, F), BF16),
            pltpu.VMEM((C, F), BF16),
            vector, vector, vector,
            pltpu.VMEM((RB, TPR, B, B), BF16),
            pltpu.SMEM((TPR, RB), jnp.int32),
            pltpu.SMEM((RB,), jnp.int32),
            pltpu.VMEM((CP, F), F32),
            row, row, row,
            labels, labels, labels, labels, labels, labels,
            slots, small, slots, small, small,
            pltpu.VMEM((GROUP, 8, CP), F32),
            pltpu.VMEM((N // GROUP, 8, CP), F32),
            pltpu.SemaphoreType.DMA((10,)),
            pltpu.SemaphoreType.DMA,
            pltpu.SemaphoreType.DMA((8,)),
            pltpu.SemaphoreType.DMA((8,)),
        ],
        compiler_params=pltpu.CompilerParams(collective_id=0, has_side_effects=True, vmem_limit_bytes=VMEM_LIMIT),
        cost_estimate=pl.CostEstimate(
            flops=6 * RB * TPR * B * B * CP, bytes_accessed=24 * 2**20, transcendentals=(ROWS + HB * B) * CP
        ),
        name="propagate",
    )(*[pltpu.with_memory_space_constraint(x, pltpu.HBM) for x in (rows_t, counts, features, wt, bias, ema, target, tiles, cols_t, used)])


def on_device(
    features, teacher_w, teacher_b, ema_prior, target_prior, send_rows, send_count, tiles, tile_col, tile_count
):
    out_t = propagate(
        send_rows.T, send_count, features, teacher_w.T, teacher_b.reshape(1, C), ema_prior.reshape(1, C),
        target_prior.reshape(1, C), tiles, tile_col.T, tile_count,
    )
    return out_t.T


def solution(mesh):
    placed = (
        P("dom", None), P(), P(), P(), P(), P("dom", None), P("dom"),
        P("dom", None, None, None), P("dom", None), P("dom"),
    )
    return jax.shard_map(on_device, mesh=mesh, in_specs=placed, out_specs=P("dom", None), check_vma=False)
```

```python
import jax
import jax.numpy as jnp
from jax import lax
from jax.experimental import pallas as pl
from jax.experimental.pallas import tpu as pltpu
from jax.sharding import PartitionSpec as P

F = 128
C = 172
CP = 256
B = 128
RB = 64
TPR = 8
SLOT = 32
HALF = 128
PACK = 16
CHUNK = 1024
UNROLL = 16
HB = 32
ROWS = 8192
N = 128
NODES = ROWS * N

MOMENTUM = 0.7
PROPAGATE = 0.9
LOG_FLOOR = 0.0001
DEAD = 32768.0
LOW = -1e30
VMEM_LIMIT = 54 * 2**20
GANG = 8
MESH = pl.DeviceIdType.MESH
MIX = 37
EARLY = 96
GROUP = 16
F32 = jnp.float32
BF16 = jnp.bfloat16


def in_hbm():
    return pl.BlockSpec(memory_space=pltpu.HBM)


def in_vmem():
    return pl.BlockSpec(memory_space=pltpu.VMEM)


def propagate_kernel(
    rows_hbm, cnt_hbm, feat_hbm, wt_hbm, b_hbm, ema_hbm, target_hbm, tiles_hbm, col_hbm, used_hbm,
    out_ref,
    wide_a, wide_b, rows_v, rows_w, rows, cnt, feat, wt, bias, ema, target, tiles, col, used,
    wpad, bpad, epad, tpad,
    seed_a, seed_b, one_a, one_b, two_a, two_b,
    send_a, send_b, feat_recv, recv_b1, recv_b2,
    part1, part2, load_sem, flip_sem, send_sem, recv_sem,
):
    me = lax.axis_index("dom")
    next_door = lax.rem(me + 1, N)

    loads = [
        pltpu.make_async_copy(src, dst, load_sem.at[i])
        for i, (src, dst) in enumerate(
            (
                (rows_hbm, rows_v), (feat_hbm, feat), (cnt_hbm, cnt), (wt_hbm, wt), (b_hbm, bias), (ema_hbm, ema),
                (target_hbm, target), (col_hbm, col), (used_hbm, used), (tiles_hbm, tiles),
            )
        )
    ]
    for load in loads[:9]:
        load.start()

    barrier = pltpu.get_barrier_semaphore()

    def tell(k, carry):
        pl.semaphore_signal(barrier, inc=1, device_id=(lax.rem(me + k, N),), device_id_type=MESH)
        return carry

    lax.fori_loop(1, N, tell, 0)

    loads[0].wait()
    rows_w[...] = jnp.concatenate([rows_v[...], jnp.zeros((B - SLOT, N), jnp.int32)], axis=0).T
    flip = pltpu.make_async_copy(rows_w, rows, flip_sem)
    flip.start()
    loads[1].wait()

    def widen(k, carry):
        at = pl.multiple_of(k * CHUNK, CHUNK)
        wide_a[pl.ds(at, CHUNK), :] = feat[pl.ds(at, CHUNK), :].astype(F32)
        return carry

    lax.fori_loop(0, ROWS // CHUNK, widen, 0)
    for load in loads[2:9]:
        load.wait()
    flip.wait()

    def picked(wide, dest, dead):
        taken = jnp.concatenate([wide[pl.ds(rows[dest, j], 1), :] for j in range(SLOT)], axis=0)
        live = lax.broadcasted_iota(jnp.int32, (SLOT, HALF), 0) < cnt[dest]
        return jnp.where(live, taken, dead)

    def packed(values):
        lane = lax.broadcasted_iota(jnp.int32, (PACK, HALF), 1)
        return jnp.where(lane < HALF // 2, values[:PACK], pltpu.roll(values[PACK:], HALF // 2, 1))

    def turned(turn, sign):
        return lax.rem(me + N + sign * lax.rem((turn + 1) * MIX, N), N)

    def spread(make, sendbuf, landing, number, first=0, last=N):
        def gang(base, size):
            dests = [turned(base + u, 1) for u in range(size)]
            for u, dest in enumerate(dests):
                sendbuf[pl.ds(base + u, 1)] = make(dest)[None]
            for u, dest in enumerate(dests):
                pltpu.make_async_remote_copy(
                    src_ref=sendbuf.at[base + u], dst_ref=landing(base + u),
                    send_sem=send_sem.at[number], recv_sem=recv_sem.at[number],
                    device_id=(dest,), device_id_type=MESH,
                ).start()

        def several(i, carry):
            gang(i * GANG, GANG)
            return carry

        full = last // GANG - (last == N)
        lax.fori_loop(first // GANG, full, several, 0)
        if last == N:
            gang(full * GANG, GANG - 1)
        whole = sendbuf.at[pl.ds(0, last - first - (last == N))]
        return pltpu.make_async_remote_copy(
            src_ref=whole, dst_ref=whole, send_sem=send_sem.at[number], recv_sem=recv_sem.at[number],
            device_id=(next_door,), device_id_type=MESH,
        )

    block_me = RB + me // (B // SLOT)
    row_me = pl.multiple_of(lax.rem(me, B // SLOT) * SLOT, SLOT)

    def own_place(labels):
        return lambda turn: labels.at[block_me, pl.ds(row_me, SLOT), :]

    def put_own(labels, values):
        labels[pl.ds(block_me, 1), pl.ds(row_me, SLOT), :] = values[None]

    def feature_rows(dest):
        return picked(wide_a, dest, DEAD).astype(BF16)

    def rows_a(dest):
        return picked(wide_a, dest, 0.0).astype(BF16)

    def rows_b(dest):
        return packed(picked(wide_b, dest, 0.0)).astype(BF16)

    def landing(turn):
        return feat_recv.at[turn]

    feat_recv[pl.ds(N - 1, 1)] = feature_rows(me)[None]
    pl.semaphore_wait(barrier, N - 1)
    early = spread(feature_rows, send_a, landing, 0, 0, EARLY)
    loads[9].start()

    wpad[...] = jnp.zeros_like(wpad)
    wpad[pl.ds(0, C), :] = wt[...].astype(F32)
    bpad[...] = jnp.full(bpad.shape, LOW, F32)
    bpad[:, pl.ds(0, C)] = bias[...]
    epad[...] = jnp.full(epad.shape, 1.0, F32)
    epad[:, pl.ds(0, C)] = ema[...]
    tpad[...] = jnp.zeros_like(tpad)
    tpad[:, pl.ds(0, C)] = target[...]
    weights = wpad[...].astype(BF16)
    blocks = CHUNK // B

    def soft(values):
        logits = lax.dot_general(values, weights, (((1,), (1,)), ((), ())), preferred_element_type=F32) + bpad[...]
        e = jnp.exp(logits - jnp.max(logits, axis=-1, keepdims=True))
        return e * (1.0 / jnp.sum(e, axis=-1, keepdims=True))

    def local(k, acc):
        p = soft(feat[pl.ds(pl.multiple_of(k * CHUNK, CHUNK), CHUNK), :]).astype(BF16)
        seed_a[pl.ds(k * blocks, blocks)] = p[:, :HALF].reshape(blocks, B, HALF)
        seed_b[pl.ds(k * blocks, blocks)] = p[:, HALF:].reshape(blocks, B, HALF)
        return acc + jnp.sum(p.astype(F32).reshape(CHUNK // 8, 8, CP), axis=0)

    acc = lax.fori_loop(0, ROWS // CHUNK, local, jnp.zeros((8, CP), F32))

    group = me // GROUP
    place = lax.rem(me, GROUP)
    groups = N // GROUP
    part1[pl.ds(place, 1)] = acc[None]

    def send_near(k, carry):
        pltpu.make_async_remote_copy(
            src_ref=part1.at[place], dst_ref=part1.at[place], send_sem=send_sem.at[5], recv_sem=recv_sem.at[5],
            device_id=(group * GROUP + lax.rem(place + k, GROUP),), device_id_type=MESH,
        ).start()
        return carry

    lax.fori_loop(1, GROUP, send_near, 0)
    late = spread(feature_rows, send_a, landing, 7, EARLY, N)
    near = pltpu.make_async_remote_copy(
        src_ref=part1.at[pl.ds(0, GROUP - 1)], dst_ref=part1.at[pl.ds(0, GROUP - 1)],
        send_sem=send_sem.at[5], recv_sem=recv_sem.at[5], device_id=(next_door,), device_id_type=MESH,
    )

    sources = CHUNK // SLOT

    def boundary(k, carry):
        f = feat_recv[pl.ds(k * sources, sources)].reshape(CHUNK, F)
        live = f[:, :1].astype(F32) < DEAD / 2
        p = jnp.where(live, soft(f), 0.0).astype(BF16)
        for u in range(sources):
            source = turned(k * sources + u, -1)
            block = RB + source // (B // SLOT)
            row = pl.multiple_of(lax.rem(source, B // SLOT) * SLOT, SLOT)
            seed_a[pl.ds(block, 1), pl.ds(row, SLOT), :] = p[u * SLOT : (u + 1) * SLOT, :HALF][None]
            seed_b[pl.ds(block, 1), pl.ds(row, SLOT), :] = p[u * SLOT : (u + 1) * SLOT, HALF:][None]
        return carry

    for labels in (seed_a, seed_b, one_a, one_b, two_a, two_b):
        labels[pl.ds(RB + HB, 1)] = jnp.zeros((1, B, HALF), BF16)
    near.wait_recv()
    part2[pl.ds(group, 1)] = jnp.sum(part1[...], axis=0)[None]

    def send_far(k, carry):
        pltpu.make_async_remote_copy(
            src_ref=part2.at[group], dst_ref=part2.at[group], send_sem=send_sem.at[6], recv_sem=recv_sem.at[6],
            device_id=(lax.rem(group + k, groups) * GROUP + place,), device_id_type=MESH,
        ).start()
        return carry

    lax.fori_loop(1, groups, send_far, 0)
    far = pltpu.make_async_remote_copy(
        src_ref=part2.at[pl.ds(0, groups - 1)], dst_ref=part2.at[pl.ds(0, groups - 1)],
        send_sem=send_sem.at[6], recv_sem=recv_sem.at[6], device_id=(next_door,), device_id_type=MESH,
    )
    early.wait_recv()
    lax.fori_loop(0, EARLY // sources, boundary, 0)
    far.wait_recv()
    total = jnp.sum(jnp.sum(part2[...], axis=0), axis=0, keepdims=True)
    ratio = tpad[...] / (MOMENTUM * epad[...] + (1.0 - MOMENTUM) * total / NODES)

    def aligned(p_a, p_b):
        a = p_a.astype(F32) * ratio[:, :HALF]
        b = p_b.astype(F32) * ratio[:, HALF:]
        row_total = jnp.sum(a + b, axis=-1, keepdims=True)
        scale = 1.0 / jnp.where(row_total > 0.0, row_total, 1.0)
        return (a * scale).astype(BF16), (b * scale).astype(BF16)

    def align(k, carry):
        a, b = aligned(
            seed_a[pl.ds(k * blocks, blocks)].reshape(CHUNK, HALF), seed_b[pl.ds(k * blocks, blocks)].reshape(CHUNK, HALF)
        )
        seed_a[pl.ds(k * blocks, blocks)] = a.reshape(blocks, B, HALF)
        seed_b[pl.ds(k * blocks, blocks)] = b.reshape(blocks, B, HALF)
        return carry

    lax.fori_loop(0, RB * B // CHUNK, align, 0)
    late.wait_recv()
    lax.fori_loop(EARLY // sources, N // sources, boundary, 0)
    lax.fori_loop(RB * B // CHUNK, (RB + HB) * B // CHUNK, align, 0)
    loads[9].wait()

    def multiply(labels, seeds, following, wides, low=None):
        def several(i, carry):
            for u in range(UNROLL):
                r = i * UNROLL + u
                count = used[r]
                lhs = jnp.concatenate([tiles[r, t] for t in range(TPR)], axis=1)
                cols = [jnp.where(t < count, col[t, r], RB + HB) for t in range(TPR)]
                rhs = jnp.concatenate([jnp.concatenate([part[c] for part in labels], axis=1) for c in cols], axis=0)
                mixed = jnp.dot(lhs, rhs, preferred_element_type=F32)
                for q, seed in enumerate(seeds):
                    own = mixed[:, q * HALF : (q + 1) * HALF]
                    current = PROPAGATE * own + (1.0 - PROPAGATE) * seed[r].astype(F32)
                    at = pl.multiple_of(r * B, B)
                    if following:
                        wides[q][pl.ds(at, B), :] = current
                        following[q][pl.ds(r, 1)] = current.astype(BF16)[None]
                    else:
                        classes = min(HALF, C - low)
                        out_ref[pl.ds(low, classes), pl.ds(at, B)] = jnp.log(current.T[:classes] + LOG_FLOOR)
            return carry

        lax.fori_loop(0, RB // UNROLL, several, 0)

    def unpack(received, labels):
        def several(h, carry):
            x = received[pl.ds(h * (B // SLOT), B // SLOT)].astype(F32)
            left = lax.broadcasted_iota(jnp.int32, x.shape, 2) < HALF // 2
            first = jnp.where(left, x, 0.0)
            second = jnp.where(left, pltpu.roll(x, HALF // 2, 2), 0.0)
            both = jnp.concatenate([first, second], axis=1).astype(BF16)
            labels[pl.ds(RB + h, 1)] = both.reshape(1, B, HALF)
            return carry

        lax.fori_loop(0, HB, several, 0, unroll=4)

    def here(received):
        return lambda turn: received.at[me]

    multiply((seed_a, seed_b), (seed_a, seed_b), (one_a, one_b), (wide_a, wide_b))
    early.wait_send()
    late.wait_send()
    recv_b1[pl.ds(me, 1)] = rows_b(me)[None]
    sent_b1 = spread(rows_b, send_b, here(recv_b1), 2)
    put_own(one_a, rows_a(me))
    sent_a1 = spread(rows_a, send_a, own_place(one_a), 1)

    sent_b1.wait_recv()
    unpack(recv_b1, one_b)
    multiply((one_b,), (seed_b,), (two_b,), (wide_b,))
    sent_b1.wait_send()
    recv_b2[pl.ds(me, 1)] = rows_b(me)[None]
    sent_b2 = spread(rows_b, send_b, here(recv_b2), 4)
    sent_a1.wait_recv()
    multiply((one_a,), (seed_a,), (two_a,), (wide_a,))
    sent_a1.wait_send()
    put_own(two_a, rows_a(me))
    sent_a2 = spread(rows_a, send_a, own_place(two_a), 3)

    sent_b2.wait_recv()
    unpack(recv_b2, two_b)
    multiply((two_b,), (seed_b,), (), (), HALF)
    sent_a2.wait_recv()
    multiply((two_a,), (seed_a,), (), (), 0)
    for sent in (near, far, sent_b2, sent_a2):
        sent.wait_send()


def propagate(rows_t, counts, features, wt, bias, ema, target, tiles, cols_t, used):
    wide = pltpu.VMEM((ROWS, HALF), F32)
    labels = pltpu.VMEM((RB + HB + 1, B, HALF), BF16)
    slots = pltpu.VMEM((N, SLOT, HALF), BF16)
    small = pltpu.VMEM((N, PACK, HALF), BF16)
    row = pltpu.VMEM((1, CP), F32)
    vector = pltpu.VMEM((1, C), F32)
    return pl.pallas_call(
        propagate_kernel,
        out_shape=pltpu.VMEM((C, ROWS), F32),
        in_specs=[in_hbm()] * 10,
        out_specs=in_vmem(),
        scratch_shapes=[
            wide, wide,
            pltpu.VMEM((SLOT, N), jnp.int32),
            pltpu.VMEM((N, B), jnp.int32),
            pltpu.SMEM((N, B), jnp.int32),
            pltpu.SMEM((N,), jnp.int32),
            pltpu.VMEM((ROWS, F), BF16),
            pltpu.VMEM((C, F), BF16),
            vector, vector, vector,
            pltpu.VMEM((RB, TPR, B, B), BF16),
            pltpu.SMEM((TPR, RB), jnp.int32),
            pltpu.SMEM((RB,), jnp.int32),
            pltpu.VMEM((CP, F), F32),
            row, row, row,
            labels, labels, labels, labels, labels, labels,
            slots, small, slots, small, small,
            pltpu.VMEM((GROUP, 8, CP), F32),
            pltpu.VMEM((N // GROUP, 8, CP), F32),
            pltpu.SemaphoreType.DMA((10,)),
            pltpu.SemaphoreType.DMA,
            pltpu.SemaphoreType.DMA((8,)),
            pltpu.SemaphoreType.DMA((8,)),
        ],
        compiler_params=pltpu.CompilerParams(collective_id=0, has_side_effects=True, vmem_limit_bytes=VMEM_LIMIT),
        cost_estimate=pl.CostEstimate(
            flops=6 * RB * TPR * B * B * CP, bytes_accessed=24 * 2**20, transcendentals=(ROWS + HB * B) * CP
        ),
        name="propagate",
    )(*[pltpu.with_memory_space_constraint(x, pltpu.HBM) for x in (rows_t, counts, features, wt, bias, ema, target, tiles, cols_t, used)])


def on_device(
    features, teacher_w, teacher_b, ema_prior, target_prior, send_rows, send_count, tiles, tile_col, tile_count
):
    out_t = propagate(
        send_rows.T, send_count, features, teacher_w.T, teacher_b.reshape(1, C), ema_prior.reshape(1, C),
        target_prior.reshape(1, C), tiles, tile_col.T, tile_count,
    )
    return out_t.T


def solution(mesh):
    placed = (
        P("dom", None), P(), P(), P(), P(), P("dom", None), P("dom"),
        P("dom", None, None, None), P("dom", None), P("dom"),
    )
    return jax.shard_map(on_device, mesh=mesh, in_specs=placed, out_specs=P("dom", None), check_vma=False)
```
